256 devices in a mesh: pop: 32 (over z, x_hi, core), hid: 8 (over y, x_lo).
Axes of the slice: x: 4 (x_hi: 2, x_lo: 2; x = x_hi * 2 + x_lo), y: 4, z: 8, core: 2. Of those that a mesh axis runs over, the one named last changes fastest.
Arguments:
- tokens: bfloat16 [1024, 4096], P('pop', 'hid'), may hold values from -6 to 6
- fitness_ranks: int32 [64], replicated, may hold values from 0 to 63, each once
- gate_weight: bfloat16 [4096, 16384], P('hid', 'pop'), may hold values from -0.09375 to 0.09375
- up_weight: bfloat16 [4096, 16384], P('hid', 'pop'), may hold values from -0.09375 to 0.09375
- down_weight: bfloat16 [16384, 4096], P('pop', 'hid'), may hold values from -0.046875 to 0.046875
- gate_input_factor: bfloat16 [64, 4, 4096], P(None, None, 'hid'), may hold values from -6 to 6
- up_input_factor: bfloat16 [64, 4, 4096], P(None, None, 'hid'), may hold values from -6 to 6
- down_right: bfloat16 [64, 4, 4096], P(None, None, 'hid'), may hold values from -6 to 6
- gate_output_factor: bfloat16 [64, 4, 16384], P('pop'), may hold values from -6 to 6
- up_output_factor: bfloat16 [64, 4, 16384], P('pop'), may hold values from -6 to 6
- down_left: bfloat16 [64, 4, 16384], P('pop'), may hold values from -6 to 6
Outputs:
- mixed: bfloat16 [1024, 4096], P('pop', 'hid')
- gate_step: float32 [4096, 16384], P('hid', 'pop')
- up_step: float32 [4096, 16384], P('hid', 'pop')
- down_step: float32 [16384, 4096], P('pop', 'hid')
The draws below stay inside these ranges and needn't reach their ends.
Inputs may be any that keep to these rules, and one draw needn't show every extreme that they name: `fitness_ranks`: every rank appears exactly once.
All inputs are finite; a program needn't handle non-finite values.
Results may differ from the reference program's by a relative error of at most 0.025.
Values may be sent and summed in bfloat16 or wider, within the bound.
A program may use at most 64 MiB of HBM per device.

```python
import math
import jax
import jax.numpy as jnp
from jax import lax

MODEL_WIDTH = 4096
HIDDEN_UNITS = 16384
RANK = 4
SAMPLE_LENGTH = 16
CANDIDATE_NUMBER = 64
TOTAL_TOKENS = 1024
N_POP = 32


def steps_of(rng, shape, split, low, high):
    def one(axis_at, shards_of):
        heights = jax.random.uniform(jax.random.fold_in(jax.random.fold_in(rng, 6), axis_at), (shards_of,), jnp.float32, low / len(split), high / len(split))
        return jnp.repeat(jnp.exp(heights), shape[axis_at] // shards_of).reshape((-1,) + (1,) * (len(shape) - axis_at - 1))

    gain = one(*split[0])
    for cut in split[1:]:
        gain = gain * one(*cut)
    return gain


def noise(own_key, extent, scale, reach, split=(), kind=jnp.bfloat16):
    factor_of = steps_of(own_key, extent, split, -0.22, 0.18) if split else 1.0
    array = jax.random.normal(own_key, extent, jnp.float32) * scale * factor_of
    return jnp.minimum(jnp.maximum(array, -reach), reach).astype(kind)


def setup_inputs(seed: int = 0) -> dict:
    streams_of = jax.random.split(jax.random.key(seed), 12)
    tokens = noise(streams_of[0], (TOTAL_TOKENS, MODEL_WIDTH), 1.0, 6.0, ((0, 32), (1, 8)))
    fitness_ranks = jax.random.permutation(streams_of[1], CANDIDATE_NUMBER).astype(jnp.int32)
    gate_weight = noise(streams_of[2], (MODEL_WIDTH, HIDDEN_UNITS), MODEL_WIDTH ** -0.5, 0.09375, ((0, 8), (1, 32)))
    up_weight = noise(streams_of[3], (MODEL_WIDTH, HIDDEN_UNITS), MODEL_WIDTH ** -0.5, 0.09375, ((0, 8), (1, 32)))
    down_weight = noise(streams_of[4], (HIDDEN_UNITS, MODEL_WIDTH), HIDDEN_UNITS ** -0.5, 0.046875, ((0, 32), (1, 8)))
    gate_input_factor = noise(streams_of[5], (CANDIDATE_NUMBER, RANK, MODEL_WIDTH), 1.0, 6.0, ((2, 8),))
    up_input_factor = noise(streams_of[6], (CANDIDATE_NUMBER, RANK, MODEL_WIDTH), 1.0, 6.0, ((2, 8),))
    down_right = noise(streams_of[7], (CANDIDATE_NUMBER, RANK, MODEL_WIDTH), 1.0, 6.0, ((2, 8),))
    gate_output_factor = noise(streams_of[8], (CANDIDATE_NUMBER, RANK, HIDDEN_UNITS), 1.0, 6.0, ((0, 32),))
    up_output_factor = noise(streams_of[9], (CANDIDATE_NUMBER, RANK, HIDDEN_UNITS), 1.0, 6.0, ((0, 32),))
    down_left = noise(streams_of[10], (CANDIDATE_NUMBER, RANK, HIDDEN_UNITS), 1.0, 6.0, ((0, 32),))
    return dict(tokens=tokens, fitness_ranks=fitness_ranks, gate_weight=gate_weight, up_weight=up_weight, down_weight=down_weight, gate_input_factor=gate_input_factor, up_input_factor=up_input_factor, down_right=down_right, gate_output_factor=gate_output_factor, up_output_factor=up_output_factor, down_left=down_left)


def reference(tokens, fitness_ranks, gate_weight, up_weight, down_weight, gate_input_factor, up_input_factor, down_right, gate_output_factor, up_output_factor, down_left):
    scalar_real = jnp.float32
    fitness = fitness_ranks.astype(scalar_real) / (CANDIDATE_NUMBER - 1) - 0.5
    scale_in = 0.5 / math.sqrt(MODEL_WIDTH * RANK)
    scale_out = 0.5 / math.sqrt(HIDDEN_UNITS * RANK)
    member_wise = tokens.reshape(CANDIDATE_NUMBER, SAMPLE_LENGTH, MODEL_WIDTH).astype(scalar_real)
    gate_projection = jnp.einsum('otl,ozl->otz', member_wise, gate_input_factor.astype(scalar_real))
    up_projection = jnp.einsum('otl,ozl->otz', member_wise, up_input_factor.astype(scalar_real))
    gate_lowrank_term = jnp.einsum('iln,ina->ila', gate_projection, gate_output_factor.astype(scalar_real)).reshape(TOTAL_TOKENS, HIDDEN_UNITS)
    gate = jnp.dot(tokens, gate_weight, preferred_element_type=scalar_real) + scale_in * gate_lowrank_term
    up_lowrank_term = jnp.einsum('iln,ina->ila', up_projection, up_output_factor.astype(scalar_real)).reshape(TOTAL_TOKENS, HIDDEN_UNITS)
    up = jnp.dot(tokens, up_weight, preferred_element_type=scalar_real) + scale_in * up_lowrank_term
    hidden = (jax.nn.silu(gate) * up).astype(jnp.bfloat16)
    embedding_dimension = HIDDEN_UNITS // N_POP
    output_factor_single = down_right.astype(scalar_real)

    def add_block(block, total):
        start = (block * embedding_dimension).astype(jnp.int32)
        zero = jnp.int32(0)
        inner_feature_slab = lax.dynamic_slice(hidden, (zero, start), (TOTAL_TOKENS, embedding_dimension))
        weight_block = lax.dynamic_slice(down_weight, (start, zero), (embedding_dimension, MODEL_WIDTH))
        left_matrix_slab = lax.dynamic_slice(down_left, (zero, zero, start), (CANDIDATE_NUMBER, RANK, embedding_dimension))
        contracting_matrix = jnp.einsum('reu,ryu->rey', inner_feature_slab.reshape(CANDIDATE_NUMBER, SAMPLE_LENGTH, embedding_dimension).astype(scalar_real), left_matrix_slab.astype(scalar_real))
        lowrank_product = jnp.einsum('okw,owt->okt', contracting_matrix, output_factor_single).reshape(TOTAL_TOKENS, MODEL_WIDTH)
        term = jnp.dot(inner_feature_slab, weight_block, preferred_element_type=scalar_real) + scale_out * lowrank_product
        rounded = lax.optimization_barrier(term.astype(jnp.bfloat16))
        return total + rounded.astype(scalar_real)
    summed = lax.fori_loop(0, N_POP, add_block, jnp.zeros((TOTAL_TOKENS, MODEL_WIDTH), scalar_real))
    mixed = summed.astype(jnp.bfloat16)
    factor = 1.0 / math.sqrt(CANDIDATE_NUMBER * RANK)
    weights3 = fitness[:, None, None]
    scaled_gate = (gate_input_factor.astype(scalar_real) * weights3).astype(jnp.bfloat16).reshape(CANDIDATE_NUMBER * RANK, MODEL_WIDTH)
    scaled_up = (up_input_factor.astype(scalar_real) * weights3).astype(jnp.bfloat16).reshape(CANDIDATE_NUMBER * RANK, MODEL_WIDTH)
    scaled_down = (down_right.astype(scalar_real) * weights3).astype(jnp.bfloat16).reshape(CANDIDATE_NUMBER * RANK, MODEL_WIDTH)
    dims = (((0,), (0,)), ((), ()))
    gate_step = factor * lax.dot_general(scaled_gate, gate_output_factor.reshape(CANDIDATE_NUMBER * RANK, HIDDEN_UNITS), dims, preferred_element_type=scalar_real)
    up_step = factor * lax.dot_general(scaled_up, up_output_factor.reshape(CANDIDATE_NUMBER * RANK, HIDDEN_UNITS), dims, preferred_element_type=scalar_real)
    down_step = factor * lax.dot_general(down_left.reshape(CANDIDATE_NUMBER * RANK, HIDDEN_UNITS), scaled_down, dims, preferred_element_type=scalar_real)
    return (mixed, gate_step, up_step, down_step)
```

```python
import functools
import math

import jax
import jax.numpy as jnp
from jax import lax
from jax.experimental import pallas as pl
from jax.experimental.pallas import tpu as pltpu
from jax.sharding import PartitionSpec as P

MODEL_WIDTH = 4096
HIDDEN_UNITS = 16384
RANK = 4
MEMBERS = 64
S_IN = 0.5 / math.sqrt(MODEL_WIDTH * RANK)
S_OUT = 0.5 / math.sqrt(HIDDEN_UNITS * RANK)
C_STEP = 1.0 / math.sqrt(MEMBERS * RANK)
MESH = pl.DeviceIdType.MESH
F32, BF16 = jnp.float32, jnp.bfloat16
OFF = (0, 1, 2, 3)
ORDER = (
    "P0", "P1", "P2", "P3", "W0", "W1", "Q0", "Q1", "Q2", "Q3",
    "T0", "T1", "B0", "T2", "B1", "T3", "B2", "B3", "C0", "C1",
    "C2", "C3", "U0", "U1", "U2", "U3", "D0", "D1", "D2", "D3",
    "E0", "E1", "E2", "E3", "R0", "R1", "R2", "R3", "F0", "F1",
    "F2", "F3", "K0", "K1", "K2", "K3", "X0", "S0", "S1", "G0",
)
X_FIRST = (True, False, True, False)


def kernel(
    ranks,
    tokens,
    gate_w,
    up_w,
    down_w,
    gate_in,
    up_in,
    down_right,
    gate_out,
    up_out,
    down_left,
    terms,
    left,
    right,
    wgu,
    wd,
    tok,
    infac,
    outfac,
    facz,
    fach,
    facd,
    facx,
    part,
    rs1,
    rsx,
    rsy,
    rs2s,
    rs2r,
    gsum,
    hid,
    tsx,
    trx,
    tacc,
    tsz,
    trz,
    scaled,
    load_sem,
    w_s,
    w_r,
    tok_s,
    tok_r,
    th_s,
    th_r,
    fz_s,
    fz_r,
    fh_s,
    fh_r,
    core_s,
    core_r,
    r1_s,
    r1_r,
    r2_s,
    r2_r,
    hx_s,
    hx_r,
    hy_s,
    hy_r,
    tx_s,
    tx_r,
    tz_s,
    tz_r,
    out_sem,
):
    pop, hdx = lax.axis_index("pop"), lax.axis_index("hid")
    z, xh, c = pop // 4, (pop // 2) % 2, pop % 2
    y, xl = hdx // 2, hdx % 2
    pair, zl = z // 2, z % 2

    def at(z_, xh_, c_, y_, xl_):
        return (z_ * 4 + xh_ * 2 + c_, y_ * 2 + xl_)

    core_peer = at(z, xh, 1 - c, y, xl)
    xl_peer = at(z, xh, c, y, 1 - xl)
    xh_peer = at(z, 1 - xh, c, y, xl)

    def y_peer(d):
        return at(z, xh, c, (y + d) % 4, xl)

    def z_others(k):
        return [1 - zl] if k == 0 else [(zl + v) % 2 for v in range(2)]

    def remote(src, dst, ss, rs, to):
        return pltpu.make_async_remote_copy(
            src_ref=src, dst_ref=dst, send_sem=ss, recv_sem=rs, device_id=to, device_id_type=MESH
        )

    def cols(n, size):
        return pl.ds(pl.multiple_of(n * size, size), size)

    sent = []

    def send(*a):
        d = remote(*a)
        d.start()
        sent.append(d)

    loads = [
        (tokens, tok.at[0, zl, xh]),
        (gate_out, outfac.at[0]),
        (up_out, outfac.at[1]),
        (down_left, outfac.at[2]),
        (gate_w, wgu.at[:, cols(c, 512)]),
        (up_w, wgu.at[:, cols(2 + c, 512)]),
        (gate_in, infac.at[0]),
        (up_in, infac.at[1]),
        (down_w, wd.at[cols(c, 512)]),
        (down_right, infac.at[2]),
    ]
    loads = [pltpu.make_async_copy(s, d, load_sem.at[i]) for i, (s, d) in enumerate(loads)]
    for d in loads:
        d.start()

    barrier = pltpu.get_barrier_semaphore()
    friends = [core_peer, xl_peer, xh_peer] + [y_peer(d) for d in (1, 2, 3)]
    for k in range(4):
        q = (pair + 4 - OFF[k]) % 4
        friends += [at(q * 2 + i, xh, c, y, xl) for i in z_others(k)]
    for f in friends:
        pl.semaphore_signal(barrier, inc=1, device_id=f, device_id_type=MESH)
    pl.semaphore_wait(barrier, len(friends))

    for d in loads[:4]:
        d.wait()

    def to_z(k):
        q = (pair + 4 - OFF[k]) % 4
        return [(v, q * 2 + i, at(q * 2 + i, xh, c, y, xl)) for v, i in enumerate(z_others(k))]

    def own_fac(a):
        return pltpu.make_async_copy(
            outfac.at[a, :, :, cols(z, 2048)], facz.at[a, 0, zl], load_sem.at[10 + a]
        )

    for a in range(3):
        own_fac(a).start()

    def send_fac(a, k, v, z_, to):
        for b in a:
            send(
                outfac.at[b, :, :, cols(z_, 2048)],
                facz.at[b, k, zl],
                fz_s.at[b, k, v],
                fz_r.at[b, k, zl],
                to,
            )

    def stage_p(k):
        for v, z_, to in to_z(k):
            send(tok.at[0, zl, xh], tok.at[k, zl, xh], tok_s.at[k, v], tok_r.at[k, zl], to)

    def stage_q(k):
        for v, z_, to in to_z(k):
            send_fac((0, 1, 2), k, v, z_, to)

    def stage_w(k):
        if k == 0:
            send(gate_w, wgu.at[:, cols(c, 512)], w_s.at[0], w_r.at[0], core_peer)
            send(up_w, wgu.at[:, cols(2 + c, 512)], w_s.at[1], w_r.at[1], core_peer)
        else:
            send(down_w, wd.at[cols(c, 512)], w_s.at[2], w_r.at[2], core_peer)

    token = lax.broadcasted_iota(jnp.int32, (128, 32), 0)
    row = lax.broadcasted_iota(jnp.int32, (128, 32), 1)
    same = (
        (token // 64 == row // 8 % 2)
        & (token // 32 % 2 == (xh + row // 16) % 2)
        & (token // 16 % 2 == row // 4 % 2)
    )

    def nt(a, b):
        return lax.dot_general(a, b, (((1,), (1,)), ((), ())), preferred_element_type=F32)

    def tn(a, b):
        return lax.dot_general(a, b, (((0,), (0,)), ((), ())), preferred_element_type=F32)

    def spread(first):
        lane = lax.broadcasted_iota(jnp.int32, (128, 32), 0)
        rank = lax.broadcasted_iota(jnp.int32, (128, 32), 1) % RANK
        return (lane == rank + first).astype(F32).astype(BF16)

    def in_rows(a, k, core):
        q = (pair + OFF[k]) % 4
        return jnp.concatenate(
            [infac[a, q, :, (xh + i) % 2, core].reshape(16, 512) for i in range(2)], axis=0
        )

    def stage_t(k):
        for i in z_others(k):
            got = tok.at[k, i, xh]
            remote(got, got, tok_s.at[k, 0], tok_r.at[k, i], core_peer).wait_recv()
        both = tok.at[k, :, xh]
        send(both, both, th_s.at[k], th_r.at[k], xh_peer)

    def stage_u(k):
        for a in range(3):
            if k == 0:
                own_fac(a).wait()
            for i in z_others(k):
                got = facz.at[a, k, i]
                remote(got, got, fz_s.at[a, k, 0], fz_r.at[a, k, i], core_peer).wait_recv()
            send(
                facz.at[a, k, :, :, :, cols(1 - xh, 1024)],
                fach.at[a, k],
                fh_s.at[a, k],
                fh_r.at[a, k],
                xh_peer,
            )

    def dense(k):
        for a in range(3):
            remote(fach.at[a, k], fach.at[a, k], fh_s.at[a, k], fh_r.at[a, k], xh_peer).wait_recv()
            own = facz[a, k, :, :, :, cols(xh, 1024)].reshape(16, 1024)
            facd[a, 32 * k : 32 * k + 16, :] = own
            facd[a, 32 * k + 16 : 32 * k + 32, :] = fach[a, k].reshape(16, 1024)

    def my_fac(a, k):
        own = facz[a, k, y // 2, xl, :, cols(xh, 1024)]
        return jnp.where(y % 2 == xh, own, fach[a, k, y // 2, xl])

    def stage_b(k):
        if k == 0:
            for i, at_ in enumerate((cols(1 - c, 512), cols(3 - c, 512))):
                remote(gate_w, wgu.at[:, at_], w_s.at[i], w_r.at[i], core_peer).wait_recv()
        both = tok.at[k, :, 1 - xh]
        remote(both, both, th_s.at[k], th_r.at[k], xh_peer).wait_recv()
        if k == 0:
            for d in loads[4:8]:
                d.wait()
        t = tok[k].reshape(128, 512)
        ext = jnp.zeros((128, 128), F32)
        for a in range(2):
            p = jnp.where(same, nt(t, in_rows(a, k, c)) * S_IN, 0.0).astype(BF16)
            ext += nt(p, spread(4 * a))
            for n in range(2):
                w = slice(1024 * a + 512 * n, 1024 * a + 512 * n + 512)
                v = jnp.dot(t, wgu[:, w], preferred_element_type=F32)
                part[k, :, :, :, w] = v.astype(BF16).reshape(4, 2, 16, 512)
        part[k, :, :, :, 2048:] = ext.astype(BF16).reshape(4, 2, 16, 128)
        if X_FIRST[k]:
            send(part.at[k, :, 1 - xl], rsx.at[k], r2_s.at[k], r2_r.at[k], xl_peer)
            return
        for d in (2, 1, 3):
            send(
                part.at[k, (y + d) % 4],
                rs1.at[k, d - 1],
                r1_s.at[k, d - 1],
                r1_r.at[k, d - 1],
                y_peer(d),
            )

    def stage_c(k):
        if X_FIRST[k]:
            remote(rsx.at[k], rsx.at[k], r2_s.at[k], r2_r.at[k], xl_peer).wait_recv()
            for d in (2, 1, 3):
                o = (y + d) % 4
                rsy[k, d - 1] = (part[k, o, xl].astype(F32) + rsx[k, o].astype(F32)).astype(BF16)
                send(
                    rsy.at[k, d - 1],
                    rs1.at[k, d - 1, 0],
                    r1_s.at[k, d - 1],
                    r1_r.at[k, d - 1],
                    y_peer(d),
                )
            gsum[k] = part[k, y, xl].astype(F32) + rsx[k, y].astype(F32)
            return
        for d in (1, 2, 3):
            remote(
                rs1.at[k, d - 1], rs1.at[k, d - 1], r1_s.at[k, d - 1], r1_r.at[k, d - 1], y_peer(d)
            ).wait_recv()

        def total(m):
            v = part[k, y, m].astype(F32)
            for d in range(3):
                v += rs1[k, d, m].astype(F32)
            return v

        rs2s[k] = total(1 - xl).astype(BF16)
        send(rs2s.at[k], rs2r.at[k], r2_s.at[k], r2_r.at[k], xl_peer)
        gsum[k] = total(xl)

    def stage_d(k):
        v = gsum[k]
        if X_FIRST[k]:
            for d in (1, 2, 3):
                got = rs1.at[k, d - 1, 0]
                remote(got, got, r1_s.at[k, d - 1], r1_r.at[k, d - 1], y_peer(d)).wait_recv()
            for d in range(3):
                v += rs1[k, d, 0].astype(F32)
        else:
            remote(rs2s.at[k], rs2r.at[k], r2_s.at[k], r2_r.at[k], xl_peer).wait_recv()
            v += rs2r[k].astype(F32)
        dense(k)
        g, u = v[:, :1024], v[:, 1024:2048]
        p = v[:, 2048:].astype(BF16)
        g += jnp.dot(p[:, :RANK], my_fac(0, k), preferred_element_type=F32)
        u += jnp.dot(p[:, RANK : 2 * RANK], my_fac(1, k), preferred_element_type=F32)
        h = (g / (1.0 + jnp.exp(-g)) * u).astype(BF16)
        hid[k, y, xl, :, :1024] = h
        p = nt(h, my_fac(2, k)) * S_OUT
        hid[k, y, xl, :, 1024:] = jnp.concatenate(
            [p.astype(BF16), jnp.zeros((16, 124), BF16)], axis=1
        )
        own = hid.at[k, y, xl]
        send(own, own, hx_s.at[k], hx_r.at[k], xl_peer)
        for d in (1, 3):
            send(own, own, hy_s.at[k, 0, d - 1], hy_r.at[k, xl, d - 1], y_peer(d))

    def stage_e(k):
        got = hid.at[k, y, 1 - xl]
        remote(got, got, hx_s.at[k], hx_r.at[k], xl_peer).wait_recv()
        for d in (1, 3):
            send(got, got, hy_s.at[k, 1, d - 1], hy_r.at[k, 1 - xl, d - 1], y_peer(d))

    def from_y(k, m, d):
        got = hid.at[k, (y + 4 - d) % 4, m]
        remote(got, got, hy_s.at[k, 0, 0], hy_r.at[k, m, d - 1], y_peer(d)).wait_recv()
        return got

    def stage_r(k):
        for m, d in ((0, 1), (1, 3)):
            got = from_y(k, m, d)
            send(got, got, hy_s.at[k, m, 1], hy_r.at[k, m, 1], y_peer(d))

    def stage_f(k):
        if k == 0:
            remote(
                down_w, wd.at[cols(1 - c, 512)], w_s.at[2], w_r.at[2], core_peer
            ).wait_recv()
            for d in loads[8:]:
                d.wait()
        for m, d in ((0, 3), (1, 1), (0, 2), (1, 2)):
            from_y(k, m, d)
        h = hid[k].reshape(128, 1152)
        p = jnp.dot(h[:, 1024:], spread(0), preferred_element_type=F32)
        p = jnp.where(same, p, 0.0).astype(BF16)
        v = jnp.dot(h[:, :1024], wd[...], preferred_element_type=F32)
        v += jnp.dot(p, in_rows(2, k, c), preferred_element_type=F32)
        v = v.reshape(2, 2, 32, 512)

        def rows(away):
            return jnp.where(xh == away, v[:, 1], v[:, 0])

        tsx[k] = rows(0).astype(BF16)
        tacc[k] = rows(1)
        send(tsx.at[k], trx.at[k], tx_s.at[k], tx_r.at[k], xh_peer)

    def stage_k(k):
        remote(tsx.at[k], trx.at[k], tx_s.at[k], tx_r.at[k], xh_peer).wait_recv()
        tsz[k] = (tacc[k] + trx[k].astype(F32)).astype(BF16)
        q = (pair + OFF[k]) % 4
        for v, i in enumerate(z_others(k)):
            to = at(q * 2 + i, xh, c, y, xl)
            send(tsz.at[k, i], trz.at[k, zl], tz_s.at[k, v], tz_r.at[k, zl], to)

    def stage_x():
        for a in range(3):
            send(
                facd.at[a, :, cols(1 - c, 512)],
                facx.at[a],
                core_s.at[a],
                core_r.at[a],
                core_peer,
            )

    def outs(a):
        return [
            pltpu.make_async_copy(facd.at[a, :, cols(c, 512)], left.at[a, 0], out_sem.at[a, 0]),
            pltpu.make_async_copy(facx.at[a], left.at[a, 1], out_sem.at[a, 1]),
            pltpu.make_async_copy(scaled.at[a], right.at[a], out_sem.at[a, 2]),
        ]

    def stage_s(part_):
        member = lax.broadcasted_iota(jnp.int32, (32, 1), 0) // 4
        if part_ == 1:
            for a in range(3):
                remote(
                    facx.at[a], facx.at[a], core_s.at[a], core_r.at[a], core_peer
                ).wait_recv()
                for d in outs(a):
                    d.start()
            return
        for k in range(4):
            for i in range(2):
                core = (c + i) % 2
                q = (pair + OFF[k]) % 4
                r = jnp.zeros((32, 1), F32)
                for m in range(8):
                    who = q * 16 + (m // 2 % 2) * 8 + core * 2 + m % 2
                    who += 4 * ((xh + m // 4) % 2)
                    r = jnp.where(member == m, ranks[who].astype(F32), r)
                fit = r / (MEMBERS - 1.0) - 0.5
                for a in range(3):
                    scaled[a, i, 32 * k : 32 * k + 32, :] = (
                        in_rows(a, k, core).astype(F32) * fit
                    ).astype(BF16)

    def stage_g():
        own = pltpu.make_async_copy(tsz.at[0, zl], trz.at[0, zl], load_sem.at[13])
        own.start()
        for k in range(4):
            for i in z_others(k):
                got = trz.at[k, i]
                remote(got, got, tz_s.at[k, 0], tz_r.at[k, i], core_peer).wait_recv()
        own.wait()
        done = pltpu.make_async_copy(trz, terms, load_sem.at[14])
        done.start()
        for a in range(3):
            for d in outs(a):
                d.wait()
        done.wait()

    stages = dict(P=stage_p, Q=stage_q, W=stage_w, T=stage_t, U=stage_u, B=stage_b)
    stages.update(C=stage_c, D=stage_d, E=stage_e, R=stage_r, F=stage_f, K=stage_k, S=stage_s)
    final = dict(X=stage_x, G=stage_g)
    for name in ORDER:
        if name[0] in stages:
            stages[name[0]](int(name[1]))
        else:
            final[name[0]]()
    for d in sent:
        d.wait_send()


def finish(terms, left, right, mixed, gate_step, up_step, down_step, tv, lv, rv, steps, in_sem, sem):
    loads = [
        (pltpu.make_async_copy(left.at[a], lv.at[a], in_sem.at[a, 0]),
         pltpu.make_async_copy(right.at[a], rv.at[a], in_sem.at[a, 1]))
        for a in range(3)
    ]
    last = pltpu.make_async_copy(terms, tv, in_sem.at[3, 0])
    for l, r in loads:
        l.start()
        r.start()
    last.start()
    copies = []
    for a, out in enumerate((gate_step, up_step, down_step)):
        for d in loads[a]:
            d.wait()
        x, y = (rv, lv) if a < 2 else (lv, rv)
        steps[a] = C_STEP * lax.dot_general(
            x[a], y[a], (((0,), (0,)), ((), ())), preferred_element_type=F32
        )
        copies.append(pltpu.make_async_copy(steps.at[a], out, sem.at[a]))
        copies[a].start()
    last.wait()
    v = tv[0].astype(F32)
    for i in range(1, 8):
        v += tv[i].astype(F32)
    mixed[...] = v.astype(BF16)
    for d in copies:
        d.wait()


def local(
    tokens,
    fitness_ranks,
    gate_weight,
    up_weight,
    down_weight,
    gate_input_factor,
    up_input_factor,
    down_right,
    gate_output_factor,
    up_output_factor,
    down_left,
):
    def grouped(x):
        return x.reshape(4, 2, 2, 2, 2, RANK, 512)

    dma = pltpu.SemaphoreType.DMA
    big = jax.ShapeDtypeStruct((512, 512), F32)
    any_ = pl.BlockSpec(memory_space=pl.ANY)
    terms, left, right = (
        pl.pallas_call(
            kernel,
            out_shape=(
                jax.ShapeDtypeStruct((4, 2, 32, 512), BF16),
                jax.ShapeDtypeStruct((3, 2, 128, 512), BF16),
                jax.ShapeDtypeStruct((3, 2, 128, 512), BF16),
            ),
            in_specs=[pl.BlockSpec(memory_space=pltpu.SMEM)] + [any_] * 10,
            out_specs=(any_, any_, any_),
            scratch_shapes=[
                pltpu.VMEM((512, 2048), BF16),
                pltpu.VMEM((1024, 512), BF16),
                pltpu.VMEM((4, 2, 2, 32, 512), BF16),
                pltpu.VMEM((3, 4, 2, 2, 2, 2, RANK, 512), BF16),
                pltpu.VMEM((3, 2, RANK, HIDDEN_UNITS), BF16),
                pltpu.VMEM((3, 4, 2, 2, RANK, 2048), BF16),
                pltpu.VMEM((3, 4, 2, 2, RANK, 1024), BF16),
                pltpu.VMEM((3, 128, 1024), BF16),
                pltpu.VMEM((3, 128, 512), BF16),
                pltpu.VMEM((4, 4, 2, 16, 2176), BF16),
                pltpu.VMEM((4, 3, 2, 16, 2176), BF16),
                pltpu.VMEM((4, 4, 16, 2176), BF16),
                pltpu.VMEM((4, 3, 16, 2176), BF16),
                pltpu.VMEM((4, 16, 2176), BF16),
                pltpu.VMEM((4, 16, 2176), BF16),
                pltpu.VMEM((4, 16, 2176), F32),
                pltpu.VMEM((4, 4, 2, 16, 1152), BF16),
                pltpu.VMEM((4, 2, 32, 512), BF16),
                pltpu.VMEM((4, 2, 32, 512), BF16),
                pltpu.VMEM((4, 2, 32, 512), F32),
                pltpu.VMEM((4, 2, 32, 512), BF16),
                pltpu.VMEM((4, 2, 32, 512), BF16),
                pltpu.VMEM((3, 2, 128, 512), BF16),
                dma((15,)),
                dma((3,)),
                dma((3,)),
                dma((4, 2)),
                dma((4, 2)),
                dma((4,)),
                dma((4,)),
                dma((3, 4, 2)),
                dma((3, 4, 2)),
                dma((3, 4)),
                dma((3, 4)),
                dma((3,)),
                dma((3,)),
                dma((4, 3)),
                dma((4, 3)),
                dma((4,)),
                dma((4,)),
                dma((4,)),
                dma((4,)),
                dma((4, 2, 3)),
                dma((4, 2, 3)),
                dma((4,)),
                dma((4,)),
                dma((4, 2)),
                dma((4, 2)),
                dma((3, 3)),
            ],
            compiler_params=pltpu.CompilerParams(
                collective_id=0, has_side_effects=True, vmem_limit_bytes=56 * 2**20
            ),
        )(
            fitness_ranks,
            tokens,
            gate_weight,
            up_weight,
            down_weight,
            grouped(gate_input_factor),
            grouped(up_input_factor),
            grouped(down_right),
            gate_output_factor,
            up_output_factor,
            down_left,
        )
    )
    vmem = pl.BlockSpec(memory_space=pltpu.VMEM)
    return pl.pallas_call(
        finish,
        out_shape=(jax.ShapeDtypeStruct((32, 512), BF16), big, big, big),
        in_specs=[any_] * 3,
        out_specs=(vmem, any_, any_, any_),
        scratch_shapes=[
            pltpu.VMEM((8, 32, 512), BF16),
            pltpu.VMEM((3, 256, 512), BF16),
            pltpu.VMEM((3, 256, 512), BF16),
            pltpu.VMEM((3, 512, 512), F32),
            dma((4, 2)),
            dma((3,)),
        ],
        compiler_params=pltpu.CompilerParams(vmem_limit_bytes=60 * 2**20),
    )(terms.reshape(8, 32, 512), left.reshape(3, 256, 512), right.reshape(3, 256, 512))


def solution(mesh):
    in_specs = (
        P("pop", "hid"),
        P(),
        P("hid", "pop"),
        P("hid", "pop"),
        P("pop", "hid"),
        P(None, None, "hid"),
        P(None, None, "hid"),
        P(None, None, "hid"),
        P("pop", None, None),
        P("pop", None, None),
        P("pop", None, None),
    )
    out_specs = (P("pop", "hid"), P("hid", "pop"), P("hid", "pop"), P("pop", "hid"))
    return jax.shard_map(local, mesh=mesh, in_specs=in_specs, out_specs=out_specs, check_vma=False)
```

```python
import functools
import math

import jax
import jax.numpy as jnp
from jax import lax
from jax.experimental import pallas as pl
from jax.experimental.pallas import tpu as pltpu
from jax.sharding import PartitionSpec as P

MODEL_WIDTH = 4096
HIDDEN_UNITS = 16384
RANK = 4
MEMBERS = 64
S_IN = 0.5 / math.sqrt(MODEL_WIDTH * RANK)
S_OUT = 0.5 / math.sqrt(HIDDEN_UNITS * RANK)
C_STEP = 1.0 / math.sqrt(MEMBERS * RANK)
MESH = pl.DeviceIdType.MESH
F32, BF16 = jnp.float32, jnp.bfloat16
OFF = (0, 1, 2, 3)
ORDER = (
    "P0", "P1", "P2", "P3", "W0", "W1", "Q0", "Q1", "Q2", "Q3",
    "T0", "T1", "B0", "T2", "B1", "T3", "B2", "B3", "U0", "C0",
    "U1", "C1", "U2", "C2", "U3", "C3", "D0", "D1", "D2", "D3",
    "X0", "S0", "E0", "E1", "E2", "E3", "R0", "R1", "R2", "R3",
    "F0", "F1", "F2", "F3", "S1", "K0", "K1", "K2", "K3", "G0",
)
X_FIRST = (True, False, True, False)


def kernel(
    ranks,
    tokens,
    gate_w,
    up_w,
    down_w,
    gate_in,
    up_in,
    down_right,
    gate_out,
    up_out,
    down_left,
    terms,
    made,
    wgu,
    wd,
    tok,
    infac,
    outfac,
    facz,
    fach,
    facd,
    facx,
    part,
    rs1,
    rsx,
    rsy,
    rs2s,
    rs2r,
    gsum,
    hid,
    tsx,
    trx,
    tacc,
    tsz,
    trz,
    scaled,
    steps,
    load_sem,
    w_s,
    w_r,
    tok_s,
    tok_r,
    th_s,
    th_r,
    fz_s,
    fz_r,
    fh_s,
    fh_r,
    core_s,
    core_r,
    r1_s,
    r1_r,
    r2_s,
    r2_r,
    hx_s,
    hx_r,
    hy_s,
    hy_r,
    tx_s,
    tx_r,
    tz_s,
    tz_r,
    out_sem,
):
    pop, hdx = lax.axis_index("pop"), lax.axis_index("hid")
    z, xh, c = pop // 4, (pop // 2) % 2, pop % 2
    y, xl = hdx // 2, hdx % 2
    pair, zl = z // 2, z % 2

    def at(z_, xh_, c_, y_, xl_):
        return (z_ * 4 + xh_ * 2 + c_, y_ * 2 + xl_)

    core_peer = at(z, xh, 1 - c, y, xl)
    xl_peer = at(z, xh, c, y, 1 - xl)
    xh_peer = at(z, 1 - xh, c, y, xl)

    def y_peer(d):
        return at(z, xh, c, (y + d) % 4, xl)

    def z_others(k):
        return [1 - zl] if k == 0 else [(zl + v) % 2 for v in range(2)]

    def remote(src, dst, ss, rs, to):
        return pltpu.make_async_remote_copy(
            src_ref=src, dst_ref=dst, send_sem=ss, recv_sem=rs, device_id=to, device_id_type=MESH
        )

    def cols(n, size):
        return pl.ds(pl.multiple_of(n * size, size), size)

    sent = []

    def send(*a):
        d = remote(*a)
        d.start()
        sent.append(d)

    loads = [
        (tokens, tok.at[0, zl, xh]),
        (gate_out, outfac.at[0]),
        (up_out, outfac.at[1]),
        (down_left, outfac.at[2]),
        (gate_w, wgu.at[:, cols(c, 512)]),
        (up_w, wgu.at[:, cols(2 + c, 512)]),
        (gate_in, infac.at[0]),
        (up_in, infac.at[1]),
        (down_w, wd.at[cols(c, 512)]),
        (down_right, infac.at[2]),
    ]
    loads = [pltpu.make_async_copy(s, d, load_sem.at[i]) for i, (s, d) in enumerate(loads)]
    for d in loads:
        d.start()

    barrier = pltpu.get_barrier_semaphore()
    friends = [core_peer, xl_peer, xh_peer] + [y_peer(d) for d in (1, 2, 3)]
    for k in range(4):
        q = (pair + 4 - OFF[k]) % 4
        friends += [at(q * 2 + i, xh, c, y, xl) for i in z_others(k)]
    for f in friends:
        pl.semaphore_signal(barrier, inc=1, device_id=f, device_id_type=MESH)
    pl.semaphore_wait(barrier, len(friends))

    for d in loads[:4]:
        d.wait()

    def to_z(k):
        q = (pair + 4 - OFF[k]) % 4
        return [(v, q * 2 + i, at(q * 2 + i, xh, c, y, xl)) for v, i in enumerate(z_others(k))]

    def own_fac(a):
        return pltpu.make_async_copy(
            outfac.at[a, :, :, cols(z, 2048)], facz.at[a, 0, zl], load_sem.at[10 + a]
        )

    for a in range(3):
        own_fac(a).start()

    def send_fac(a, k, v, z_, to):
        for b in a:
            send(
                outfac.at[b, :, :, cols(z_, 2048)],
                facz.at[b, k, zl],
                fz_s.at[b, k, v],
                fz_r.at[b, k, zl],
                to,
            )

    def stage_p(k):
        for v, z_, to in to_z(k):
            send(tok.at[0, zl, xh], tok.at[k, zl, xh], tok_s.at[k, v], tok_r.at[k, zl], to)

    def stage_q(k):
        for v, z_, to in to_z(k):
            send_fac((0, 1, 2), k, v, z_, to)

    def stage_w(k):
        if k == 0:
            send(gate_w, wgu.at[:, cols(c, 512)], w_s.at[0], w_r.at[0], core_peer)
            send(up_w, wgu.at[:, cols(2 + c, 512)], w_s.at[1], w_r.at[1], core_peer)
        else:
            send(down_w, wd.at[cols(c, 512)], w_s.at[2], w_r.at[2], core_peer)

    token = lax.broadcasted_iota(jnp.int32, (128, 32), 0)
    row = lax.broadcasted_iota(jnp.int32, (128, 32), 1)
    same = (
        (token // 64 == row // 8 % 2)
        & (token // 32 % 2 == (xh + row // 16) % 2)
        & (token // 16 % 2 == row // 4 % 2)
    )

    def nt(a, b):
        return lax.dot_general(a, b, (((1,), (1,)), ((), ())), preferred_element_type=F32)

    def tn(a, b):
        return lax.dot_general(a, b, (((0,), (0,)), ((), ())), preferred_element_type=F32)

    def spread(first):
        lane = lax.broadcasted_iota(jnp.int32, (128, 32), 0)
        rank = lax.broadcasted_iota(jnp.int32, (128, 32), 1) % RANK
        return (lane == rank + first).astype(F32).astype(BF16)

    def in_rows(a, k, core):
        q = (pair + OFF[k]) % 4
        return jnp.concatenate(
            [infac[a, q, :, (xh + i) % 2, core].reshape(16, 512) for i in range(2)], axis=0
        )

    def stage_t(k):
        for i in z_others(k):
            got = tok.at[k, i, xh]
            remote(got, got, tok_s.at[k, 0], tok_r.at[k, i], core_peer).wait_recv()
        both = tok.at[k, :, xh]
        send(both, both, th_s.at[k], th_r.at[k], xh_peer)

    def stage_u(k):
        for a in range(3):
            if k == 0:
                own_fac(a).wait()
            for i in z_others(k):
                got = facz.at[a, k, i]
                remote(got, got, fz_s.at[a, k, 0], fz_r.at[a, k, i], core_peer).wait_recv()
            send(
                facz.at[a, k, :, :, :, cols(1 - xh, 1024)],
                fach.at[a, k],
                fh_s.at[a, k],
                fh_r.at[a, k],
                xh_peer,
            )

    def other_half(k):
        for a in range(3):
            remote(fach.at[a, k], fach.at[a, k], fh_s.at[a, k], fh_r.at[a, k], xh_peer).wait_recv()

    def my_fac(a, k):
        own = facz[a, k, y // 2, xl, :, cols(xh, 1024)]
        return jnp.where(y % 2 == xh, own, fach[a, k, y // 2, xl])

    def stage_b(k):
        if k == 0:
            for i, at_ in enumerate((cols(1 - c, 512), cols(3 - c, 512))):
                remote(gate_w, wgu.at[:, at_], w_s.at[i], w_r.at[i], core_peer).wait_recv()
        both = tok.at[k, :, 1 - xh]
        remote(both, both, th_s.at[k], th_r.at[k], xh_peer).wait_recv()
        if k == 0:
            for d in loads[4:]:
                d.wait()
        t = tok[k].reshape(128, 512)
        ext = jnp.zeros((128, 128), F32)
        for a in range(2):
            p = jnp.where(same, nt(t, in_rows(a, k, c)) * S_IN, 0.0).astype(BF16)
            ext += nt(p, spread(4 * a))
            for n in range(2):
                w = slice(1024 * a + 512 * n, 1024 * a + 512 * n + 512)
                v = jnp.dot(t, wgu[:, w], preferred_element_type=F32)
                part[k, :, :, :, w] = v.astype(BF16).reshape(4, 2, 16, 512)
        part[k, :, :, :, 2048:] = ext.astype(BF16).reshape(4, 2, 16, 128)
        if X_FIRST[k]:
            send(part.at[k, :, 1 - xl], rsx.at[k], r2_s.at[k], r2_r.at[k], xl_peer)
            return
        for d in (2, 1, 3):
            send(
                part.at[k, (y + d) % 4],
                rs1.at[k, d - 1],
                r1_s.at[k, d - 1],
                r1_r.at[k, d - 1],
                y_peer(d),
            )

    def stage_c(k):
        if X_FIRST[k]:
            remote(rsx.at[k], rsx.at[k], r2_s.at[k], r2_r.at[k], xl_peer).wait_recv()
            for d in (2, 1, 3):
                o = (y + d) % 4
                rsy[k, d - 1] = (part[k, o, xl].astype(F32) + rsx[k, o].astype(F32)).astype(BF16)
                send(
                    rsy.at[k, d - 1],
                    rs1.at[k, d - 1, 0],
                    r1_s.at[k, d - 1],
                    r1_r.at[k, d - 1],
                    y_peer(d),
                )
            gsum[k] = part[k, y, xl].astype(F32) + rsx[k, y].astype(F32)
            return
        for d in (1, 2, 3):
            remote(
                rs1.at[k, d - 1], rs1.at[k, d - 1], r1_s.at[k, d - 1], r1_r.at[k, d - 1], y_peer(d)
            ).wait_recv()

        def total(m):
            v = part[k, y, m].astype(F32)
            for d in range(3):
                v += rs1[k, d, m].astype(F32)
            return v

        rs2s[k] = total(1 - xl).astype(BF16)
        send(rs2s.at[k], rs2r.at[k], r2_s.at[k], r2_r.at[k], xl_peer)
        gsum[k] = total(xl)

    def stage_d(k):
        v = gsum[k]
        if X_FIRST[k]:
            for d in (1, 2, 3):
                got = rs1.at[k, d - 1, 0]
                remote(got, got, r1_s.at[k, d - 1], r1_r.at[k, d - 1], y_peer(d)).wait_recv()
            for d in range(3):
                v += rs1[k, d, 0].astype(F32)
        else:
            remote(rs2s.at[k], rs2r.at[k], r2_s.at[k], r2_r.at[k], xl_peer).wait_recv()
            v += rs2r[k].astype(F32)
        other_half(k)
        g, u = v[:, :1024], v[:, 1024:2048]
        p = v[:, 2048:].astype(BF16)
        g += jnp.dot(p[:, :RANK], my_fac(0, k), preferred_element_type=F32)
        u += jnp.dot(p[:, RANK : 2 * RANK], my_fac(1, k), preferred_element_type=F32)
        h = (g / (1.0 + jnp.exp(-g)) * u).astype(BF16)
        hid[k, y, xl, :, :1024] = h
        p = nt(h, my_fac(2, k)) * S_OUT
        hid[k, y, xl, :, 1024:] = jnp.concatenate(
            [p.astype(BF16), jnp.zeros((16, 124), BF16)], axis=1
        )
        own = hid.at[k, y, xl]
        send(own, own, hx_s.at[k], hx_r.at[k], xl_peer)
        for d in (1, 3):
            send(own, own, hy_s.at[k, 0, d - 1], hy_r.at[k, xl, d - 1], y_peer(d))

    def stage_e(k):
        got = hid.at[k, y, 1 - xl]
        remote(got, got, hx_s.at[k], hx_r.at[k], xl_peer).wait_recv()
        for d in (1, 3):
            send(got, got, hy_s.at[k, 1, d - 1], hy_r.at[k, 1 - xl, d - 1], y_peer(d))

    def from_y(k, m, d):
        got = hid.at[k, (y + 4 - d) % 4, m]
        remote(got, got, hy_s.at[k, 0, 0], hy_r.at[k, m, d - 1], y_peer(d)).wait_recv()
        return got

    def stage_r(k):
        for m, d in ((0, 1), (1, 3)):
            got = from_y(k, m, d)
            send(got, got, hy_s.at[k, m, 1], hy_r.at[k, m, 1], y_peer(d))

    def stage_f(k):
        if k == 0:
            remote(
                down_w, wd.at[cols(1 - c, 512)], w_s.at[2], w_r.at[2], core_peer
            ).wait_recv()
        for m, d in ((0, 3), (1, 1), (0, 2), (1, 2)):
            from_y(k, m, d)
        h = hid[k].reshape(128, 1152)
        p = jnp.dot(h[:, 1024:], spread(0), preferred_element_type=F32)
        p = jnp.where(same, p, 0.0).astype(BF16)
        v = jnp.dot(h[:, :1024], wd[...], preferred_element_type=F32)
        v += jnp.dot(p, in_rows(2, k, c), preferred_element_type=F32)
        v = v.reshape(2, 2, 32, 512)

        def rows(away):
            return jnp.where(xh == away, v[:, 1], v[:, 0])

        tsx[k] = rows(0).astype(BF16)
        tacc[k] = rows(1)
        send(tsx.at[k], trx.at[k], tx_s.at[k], tx_r.at[k], xh_peer)

    def stage_k(k):
        remote(tsx.at[k], trx.at[k], tx_s.at[k], tx_r.at[k], xh_peer).wait_recv()
        tsz[k] = (tacc[k] + trx[k].astype(F32)).astype(BF16)
        q = (pair + OFF[k]) % 4
        for v, i in enumerate(z_others(k)):
            to = at(q * 2 + i, xh, c, y, xl)
            send(tsz.at[k, i], trz.at[k, zl], tz_s.at[k, v], tz_r.at[k, zl], to)

    def stage_x():
        for a in range(3):
            for k in range(4):
                own = facz[a, k, :, :, :, cols(xh, 1024)].reshape(16, 1024)
                facd[a, 32 * k : 32 * k + 16, :] = own
                facd[a, 32 * k + 16 : 32 * k + 32, :] = fach[a, k].reshape(16, 1024)
            send(
                facd.at[a, :, cols(1 - c, 512)],
                facx.at[a],
                core_s.at[a],
                core_r.at[a],
                core_peer,
            )

    def outs(a):
        return pltpu.make_async_copy(steps.at[a], made.at[a], out_sem.at[a])

    def stage_s(part_):
        member = lax.broadcasted_iota(jnp.int32, (32, 1), 0) // 4
        if part_ == 1:
            for a in range(3):
                remote(
                    facx.at[a], facx.at[a], core_s.at[a], core_r.at[a], core_peer
                ).wait_recv()
                v = None
                for i in range(2):
                    f = facd[a, :, cols(c, 512)] if i == 0 else facx[a]
                    x = scaled[a, i]
                    w = tn(x, f) if a < 2 else tn(f, x)
                    v = w if v is None else v + w
                steps[a] = v * C_STEP
                outs(a).start()
            return
        for k in range(4):
            for i in range(2):
                core = (c + i) % 2
                q = (pair + OFF[k]) % 4
                r = jnp.zeros((32, 1), F32)
                for m in range(8):
                    who = q * 16 + (m // 2 % 2) * 8 + core * 2 + m % 2
                    who += 4 * ((xh + m // 4) % 2)
                    r = jnp.where(member == m, ranks[who].astype(F32), r)
                fit = r / (MEMBERS - 1.0) - 0.5
                for a in range(3):
                    scaled[a, i, 32 * k : 32 * k + 32, :] = (
                        in_rows(a, k, core).astype(F32) * fit
                    ).astype(BF16)

    def stage_g():
        own = pltpu.make_async_copy(tsz.at[0, zl], trz.at[0, zl], load_sem.at[13])
        own.start()
        for k in range(4):
            for i in z_others(k):
                got = trz.at[k, i]
                remote(got, got, tz_s.at[k, 0], tz_r.at[k, i], core_peer).wait_recv()
        own.wait()
        done = pltpu.make_async_copy(trz, terms, load_sem.at[14])
        done.start()
        for a in range(3):
            outs(a).wait()
        done.wait()

    stages = dict(P=stage_p, Q=stage_q, W=stage_w, T=stage_t, U=stage_u, B=stage_b)
    stages.update(C=stage_c, D=stage_d, E=stage_e, R=stage_r, F=stage_f, K=stage_k, S=stage_s)
    final = dict(X=stage_x, G=stage_g)
    for name in ORDER:
        if name[0] in stages:
            stages[name[0]](int(name[1]))
        else:
            final[name[0]]()
    for d in sent:
        d.wait_send()


def finish(terms, made, mixed, gate_step, up_step, down_step, tv, held, in_sem, sem, out_sem):
    load = pltpu.make_async_copy(terms, tv, in_sem)
    load.start()
    pieces = [(a, i, pl.ds(128 * i, 128)) for a in range(3) for i in range(4)]
    loads = [
        pltpu.make_async_copy(made.at[a, rows], held.at[a, rows], sem.at[a, i])
        for a, i, rows in pieces
    ]
    for d in loads:
        d.start()
    outs = (gate_step, up_step, down_step)
    stores = [
        pltpu.make_async_copy(held.at[a, rows], outs[a].at[rows], out_sem.at[a, i])
        for a, i, rows in pieces
    ]
    for l, d in zip(loads, stores):
        l.wait()
        d.start()
    load.wait()
    v = tv[0].astype(F32)
    for i in range(1, 8):
        v += tv[i].astype(F32)
    mixed[...] = v.astype(BF16)
    for d in stores:
        d.wait()


def local(
    tokens,
    fitness_ranks,
    gate_weight,
    up_weight,
    down_weight,
    gate_input_factor,
    up_input_factor,
    down_right,
    gate_output_factor,
    up_output_factor,
    down_left,
):
    def grouped(x):
        return x.reshape(4, 2, 2, 2, 2, RANK, 512)

    dma = pltpu.SemaphoreType.DMA
    big = jax.ShapeDtypeStruct((512, 512), F32)
    any_ = pl.BlockSpec(memory_space=pl.ANY)
    terms, made = (
        pl.pallas_call(
            kernel,
            out_shape=(
                jax.ShapeDtypeStruct((4, 2, 32, 512), BF16),
                jax.ShapeDtypeStruct((3, 512, 512), F32),
            ),
            in_specs=[pl.BlockSpec(memory_space=pltpu.SMEM)] + [any_] * 10,
            out_specs=(any_, any_),
            scratch_shapes=[
                pltpu.VMEM((512, 2048), BF16),
                pltpu.VMEM((1024, 512), BF16),
                pltpu.VMEM((4, 2, 2, 32, 512), BF16),
                pltpu.VMEM((3, 4, 2, 2, 2, 2, RANK, 512), BF16),
                pltpu.VMEM((3, 2, RANK, HIDDEN_UNITS), BF16),
                pltpu.VMEM((3, 4, 2, 2, RANK, 2048), BF16),
                pltpu.VMEM((3, 4, 2, 2, RANK, 1024), BF16),
                pltpu.VMEM((3, 128, 1024), BF16),
                pltpu.VMEM((3, 128, 512), BF16),
                pltpu.VMEM((4, 4, 2, 16, 2176), BF16),
                pltpu.VMEM((4, 3, 2, 16, 2176), BF16),
                pltpu.VMEM((4, 4, 16, 2176), BF16),
                pltpu.VMEM((4, 3, 16, 2176), BF16),
                pltpu.VMEM((4, 16, 2176), BF16),
                pltpu.VMEM((4, 16, 2176), BF16),
                pltpu.VMEM((4, 16, 2176), F32),
                pltpu.VMEM((4, 4, 2, 16, 1152), BF16),
                pltpu.VMEM((4, 2, 32, 512), BF16),
                pltpu.VMEM((4, 2, 32, 512), BF16),
                pltpu.VMEM((4, 2, 32, 512), F32),
                pltpu.VMEM((4, 2, 32, 512), BF16),
                pltpu.VMEM((4, 2, 32, 512), BF16),
                pltpu.VMEM((3, 2, 128, 512), BF16),
                pltpu.VMEM((3, 512, 512), F32),
                dma((15,)),
                dma((3,)),
                dma((3,)),
                dma((4, 2)),
                dma((4, 2)),
                dma((4,)),
                dma((4,)),
                dma((3, 4, 2)),
                dma((3, 4, 2)),
                dma((3, 4)),
                dma((3, 4)),
                dma((3,)),
                dma((3,)),
                dma((4, 3)),
                dma((4, 3)),
                dma((4,)),
                dma((4,)),
                dma((4,)),
                dma((4,)),
                dma((4, 2, 3)),
                dma((4, 2, 3)),
                dma((4,)),
                dma((4,)),
                dma((4, 2)),
                dma((4, 2)),
                dma((3,)),
            ],
            compiler_params=pltpu.CompilerParams(
                collective_id=0, has_side_effects=True, vmem_limit_bytes=56 * 2**20
            ),
        )(
            fitness_ranks,
            tokens,
            gate_weight,
            up_weight,
            down_weight,
            grouped(gate_input_factor),
            grouped(up_input_factor),
            grouped(down_right),
            gate_output_factor,
            up_output_factor,
            down_left,
        )
    )
    vmem = pl.BlockSpec(memory_space=pltpu.VMEM)
    return pl.pallas_call(
        finish,
        out_shape=(jax.ShapeDtypeStruct((32, 512), BF16), big, big, big),
        in_specs=[any_] * 2,
        out_specs=(vmem, any_, any_, any_),
        scratch_shapes=[
            pltpu.VMEM((8, 32, 512), BF16),
            pltpu.VMEM((3, 512, 512), F32),
            dma(()),
            dma((3, 4)),
            dma((3, 4)),
        ],
        compiler_params=pltpu.CompilerParams(vmem_limit_bytes=60 * 2**20),
    )(terms.reshape(8, 32, 512), made)


def solution(mesh):
    in_specs = (
        P("pop", "hid"),
        P(),
        P("hid", "pop"),
        P("hid", "pop"),
        P("pop", "hid"),
        P(None, None, "hid"),
        P(None, None, "hid"),
        P(None, None, "hid"),
        P("pop", None, None),
        P("pop", None, None),
        P("pop", None, None),
    )
    out_specs = (P("pop", "hid"), P("hid", "pop"), P("hid", "pop"), P("pop", "hid"))
    return jax.shard_map(local, mesh=mesh, in_specs=in_specs, out_specs=out_specs, check_vma=False)
```

```python
import functools
import math

import jax
import jax.numpy as jnp
from jax import lax
from jax.experimental import pallas as pl
from jax.experimental.pallas import tpu as pltpu
from jax.sharding import PartitionSpec as P

MODEL_WIDTH = 4096
HIDDEN_UNITS = 16384
RANK = 4
MEMBERS = 64
S_IN = 0.5 / math.sqrt(MODEL_WIDTH * RANK)
S_OUT = 0.5 / math.sqrt(HIDDEN_UNITS * RANK)
C_STEP = 1.0 / math.sqrt(MEMBERS * RANK)
MESH = pl.DeviceIdType.MESH
F32, BF16 = jnp.float32, jnp.bfloat16
OFF = (0, 1, 2, 3)
ORDER = (
    "P0", "P1", "P2", "P3", "W0", "W1", "Q0", "Q1", "Q2", "Q3",
    "T0", "T1", "B0", "T2", "B1", "T3", "B2", "B3", "U0", "C0",
    "U1", "C1", "U2", "C2", "U3", "C3", "D0", "D1", "D2", "D3",
    "X0", "S0", "E0", "E1", "E2", "E3", "R0", "R1", "R2", "R3",
    "F0", "F1", "F2", "F3", "S1", "K0", "K1", "K2", "K3", "G0",
)
X_FIRST = (False, False, True, False)


def kernel(
    ranks,
    tokens,
    gate_w,
    up_w,
    down_w,
    gate_in,
    up_in,
    down_right,
    gate_out,
    up_out,
    down_left,
    terms,
    made,
    wgu,
    wd,
    tok,
    infac,
    outfac,
    facz,
    fach,
    facd,
    facx,
    part,
    rs1,
    rsx,
    rsy,
    rs2s,
    rs2r,
    gsum,
    hid,
    tsx,
    trx,
    tacc,
    tsz,
    trz,
    scaled,
    steps,
    load_sem,
    w_s,
    w_r,
    tok_s,
    tok_r,
    th_s,
    th_r,
    fz_s,
    fz_r,
    fh_s,
    fh_r,
    core_s,
    core_r,
    r1_s,
    r1_r,
    r2_s,
    r2_r,
    hx_s,
    hx_r,
    hy_s,
    hy_r,
    tx_s,
    tx_r,
    tz_s,
    tz_r,
    out_sem,
):
    pop, hdx = lax.axis_index("pop"), lax.axis_index("hid")
    z, xh, c = pop // 4, (pop // 2) % 2, pop % 2
    y, xl = hdx // 2, hdx % 2
    pair, zl = z // 2, z % 2

    def at(z_, xh_, c_, y_, xl_):
        return (z_ * 4 + xh_ * 2 + c_, y_ * 2 + xl_)

    core_peer = at(z, xh, 1 - c, y, xl)
    xl_peer = at(z, xh, c, y, 1 - xl)
    xh_peer = at(z, 1 - xh, c, y, xl)

    def y_peer(d):
        return at(z, xh, c, (y + d) % 4, xl)

    def z_others(k):
        return [1 - zl] if k == 0 else [(zl + v) % 2 for v in range(2)]

    def remote(src, dst, ss, rs, to):
        return pltpu.make_async_remote_copy(
            src_ref=src, dst_ref=dst, send_sem=ss, recv_sem=rs, device_id=to, device_id_type=MESH
        )

    def cols(n, size):
        return pl.ds(pl.multiple_of(n * size, size), size)

    sent = []

    def send(*a):
        d = remote(*a)
        d.start()
        sent.append(d)

    loads = [
        (tokens, tok.at[0, zl, xh]),
        (gate_out, outfac.at[0]),
        (up_out, outfac.at[1]),
        (down_left, outfac.at[2]),
        (gate_w, wgu.at[:, cols(c, 512)]),
        (up_w, wgu.at[:, cols(2 + c, 512)]),
        (gate_in, infac.at[0]),
        (up_in, infac.at[1]),
        (down_w, wd.at[cols(c, 512)]),
        (down_right, infac.at[2]),
    ]
    loads = [pltpu.make_async_copy(s, d, load_sem.at[i]) for i, (s, d) in enumerate(loads)]
    for d in loads:
        d.start()

    barrier = pltpu.get_barrier_semaphore()
    friends = [core_peer, xl_peer, xh_peer] + [y_peer(d) for d in (1, 2, 3)]
    for k in range(4):
        q = (pair + 4 - OFF[k]) % 4
        friends += [at(q * 2 + i, xh, c, y, xl) for i in z_others(k)]
    for f in friends:
        pl.semaphore_signal(barrier, inc=1, device_id=f, device_id_type=MESH)
    pl.semaphore_wait(barrier, len(friends))

    for d in loads[:4]:
        d.wait()

    def to_z(k):
        q = (pair + 4 - OFF[k]) % 4
        return [(v, q * 2 + i, at(q * 2 + i, xh, c, y, xl)) for v, i in enumerate(z_others(k))]

    def own_fac(a):
        return pltpu.make_async_copy(
            outfac.at[a, :, :, cols(z, 2048)], facz.at[a, 0, zl], load_sem.at[10 + a]
        )

    for a in range(3):
        own_fac(a).start()

    def send_fac(a, k, v, z_, to):
        for b in a:
            send(
                outfac.at[b, :, :, cols(z_, 2048)],
                facz.at[b, k, zl],
                fz_s.at[b, k, v],
                fz_r.at[b, k, zl],
                to,
            )

    def stage_p(k):
        for v, z_, to in to_z(k):
            send(tok.at[0, zl, xh], tok.at[k, zl, xh], tok_s.at[k, v], tok_r.at[k, zl], to)

    def stage_q(k):
        for v, z_, to in to_z(k):
            send_fac((0, 1, 2), k, v, z_, to)

    def stage_w(k):
        if k == 0:
            send(gate_w, wgu.at[:, cols(c, 512)], w_s.at[0], w_r.at[0], core_peer)
            send(up_w, wgu.at[:, cols(2 + c, 512)], w_s.at[1], w_r.at[1], core_peer)
        else:
            send(down_w, wd.at[cols(c, 512)], w_s.at[2], w_r.at[2], core_peer)

    token = lax.broadcasted_iota(jnp.int32, (128, 32), 0)
    row = lax.broadcasted_iota(jnp.int32, (128, 32), 1)
    same = (
        (token // 64 == row // 8 % 2)
        & (token // 32 % 2 == (xh + row // 16) % 2)
        & (token // 16 % 2 == row // 4 % 2)
    )

    def nt(a, b):
        return lax.dot_general(a, b, (((1,), (1,)), ((), ())), preferred_element_type=F32)

    def tn(a, b):
        return lax.dot_general(a, b, (((0,), (0,)), ((), ())), preferred_element_type=F32)

    def spread(first):
        lane = lax.broadcasted_iota(jnp.int32, (128, 32), 0)
        rank = lax.broadcasted_iota(jnp.int32, (128, 32), 1) % RANK
        return (lane == rank + first).astype(F32).astype(BF16)

    def in_rows(a, k, core):
        q = (pair + OFF[k]) % 4
        return jnp.concatenate(
            [infac[a, q, :, (xh + i) % 2, core].reshape(16, 512) for i in range(2)], axis=0
        )

    def stage_t(k):
        for i in z_others(k):
            got = tok.at[k, i, xh]
            remote(got, got, tok_s.at[k, 0], tok_r.at[k, i], core_peer).wait_recv()
        both = tok.at[k, :, xh]
        send(both, both, th_s.at[k], th_r.at[k], xh_peer)

    def stage_u(k):
        for a in range(3):
            if k == 0:
                own_fac(a).wait()
            for i in z_others(k):
                got = facz.at[a, k, i]
                remote(got, got, fz_s.at[a, k, 0], fz_r.at[a, k, i], core_peer).wait_recv()
            send(
                facz.at[a, k, :, :, :, cols(1 - xh, 1024)],
                fach.at[a, k],
                fh_s.at[a, k],
                fh_r.at[a, k],
                xh_peer,
            )

    def other_half(k):
        for a in range(3):
            remote(fach.at[a, k], fach.at[a, k], fh_s.at[a, k], fh_r.at[a, k], xh_peer).wait_recv()

    def my_fac(a, k):
        own = facz[a, k, y // 2, xl, :, cols(xh, 1024)]
        return jnp.where(y % 2 == xh, own, fach[a, k, y // 2, xl])

    def stage_b(k):
        if k == 0:
            for i, at_ in enumerate((cols(1 - c, 512), cols(3 - c, 512))):
                remote(gate_w, wgu.at[:, at_], w_s.at[i], w_r.at[i], core_peer).wait_recv()
        both = tok.at[k, :, 1 - xh]
        remote(both, both, th_s.at[k], th_r.at[k], xh_peer).wait_recv()
        if k == 0:
            for d in loads[4:]:
                d.wait()
        t = tok[k].reshape(128, 512)
        ext = jnp.zeros((128, 128), F32)
        for a in range(2):
            p = jnp.where(same, nt(t, in_rows(a, k, c)) * S_IN, 0.0).astype(BF16)
            ext += nt(p, spread(4 * a))
            for n in range(2):
                w = slice(1024 * a + 512 * n, 1024 * a + 512 * n + 512)
                v = jnp.dot(t, wgu[:, w], preferred_element_type=F32)
                part[k, :, :, :, w] = v.astype(BF16).reshape(4, 2, 16, 512)
        part[k, :, :, :, 2048:] = ext.astype(BF16).reshape(4, 2, 16, 128)
        if X_FIRST[k]:
            send(part.at[k, :, 1 - xl], rsx.at[k], r2_s.at[k], r2_r.at[k], xl_peer)
            return
        for d in (2, 1, 3):
            send(
                part.at[k, (y + d) % 4],
                rs1.at[k, d - 1],
                r1_s.at[k, d - 1],
                r1_r.at[k, d - 1],
                y_peer(d),
            )

    def stage_c(k):
        if X_FIRST[k]:
            remote(rsx.at[k], rsx.at[k], r2_s.at[k], r2_r.at[k], xl_peer).wait_recv()
            for d in (2, 1, 3):
                o = (y + d) % 4
                rsy[k, d - 1] = (part[k, o, xl].astype(F32) + rsx[k, o].astype(F32)).astype(BF16)
                send(
                    rsy.at[k, d - 1],
                    rs1.at[k, d - 1, 0],
                    r1_s.at[k, d - 1],
                    r1_r.at[k, d - 1],
                    y_peer(d),
                )
            gsum[k] = part[k, y, xl].astype(F32) + rsx[k, y].astype(F32)
            return
        for d in (1, 2, 3):
            remote(
                rs1.at[k, d - 1], rs1.at[k, d - 1], r1_s.at[k, d - 1], r1_r.at[k, d - 1], y_peer(d)
            ).wait_recv()

        def total(m):
            v = part[k, y, m].astype(F32)
            for d in range(3):
                v += rs1[k, d, m].astype(F32)
            return v

        rs2s[k] = total(1 - xl).astype(BF16)
        send(rs2s.at[k], rs2r.at[k], r2_s.at[k], r2_r.at[k], xl_peer)
        gsum[k] = total(xl)

    def stage_d(k):
        v = gsum[k]
        if X_FIRST[k]:
            for d in (1, 2, 3):
                got = rs1.at[k, d - 1, 0]
                remote(got, got, r1_s.at[k, d - 1], r1_r.at[k, d - 1], y_peer(d)).wait_recv()
            for d in range(3):
                v += rs1[k, d, 0].astype(F32)
        else:
            remote(rs2s.at[k], rs2r.at[k], r2_s.at[k], r2_r.at[k], xl_peer).wait_recv()
            v += rs2r[k].astype(F32)
        other_half(k)
        g, u = v[:, :1024], v[:, 1024:2048]
        p = v[:, 2048:].astype(BF16)
        g += jnp.dot(p[:, :RANK], my_fac(0, k), preferred_element_type=F32)
        u += jnp.dot(p[:, RANK : 2 * RANK], my_fac(1, k), preferred_element_type=F32)
        h = (g / (1.0 + jnp.exp(-g)) * u).astype(BF16)
        hid[k, y, xl, :, :1024] = h
        p = nt(h, my_fac(2, k)) * S_OUT
        hid[k, y, xl, :, 1024:] = jnp.concatenate(
            [p.astype(BF16), jnp.zeros((16, 124), BF16)], axis=1
        )
        own = hid.at[k, y, xl]
        send(own, own, hx_s.at[k], hx_r.at[k], xl_peer)
        for d in (1, 3):
            send(own, own, hy_s.at[k, 0, d - 1], hy_r.at[k, xl, d - 1], y_peer(d))

    def stage_e(k):
        got = hid.at[k, y, 1 - xl]
        remote(got, got, hx_s.at[k], hx_r.at[k], xl_peer).wait_recv()
        for d in (1, 3):
            send(got, got, hy_s.at[k, 1, d - 1], hy_r.at[k, 1 - xl, d - 1], y_peer(d))

    def from_y(k, m, d):
        got = hid.at[k, (y + 4 - d) % 4, m]
        remote(got, got, hy_s.at[k, 0, 0], hy_r.at[k, m, d - 1], y_peer(d)).wait_recv()
        return got

    def stage_r(k):
        for m, d in ((0, 1), (1, 3)):
            got = from_y(k, m, d)
            send(got, got, hy_s.at[k, m, 1], hy_r.at[k, m, 1], y_peer(d))

    def stage_f(k):
        if k == 0:
            remote(
                down_w, wd.at[cols(1 - c, 512)], w_s.at[2], w_r.at[2], core_peer
            ).wait_recv()
        for m, d in ((0, 3), (1, 1), (0, 2), (1, 2)):
            from_y(k, m, d)
        h = hid[k].reshape(128, 1152)
        p = jnp.dot(h[:, 1024:], spread(0), preferred_element_type=F32)
        p = jnp.where(same, p, 0.0).astype(BF16)
        v = jnp.dot(h[:, :1024], wd[...], preferred_element_type=F32)
        v += jnp.dot(p, in_rows(2, k, c), preferred_element_type=F32)
        v = v.reshape(2, 2, 32, 512)

        def rows(away):
            return jnp.where(xh == away, v[:, 1], v[:, 0])

        tsx[k] = rows(0).astype(BF16)
        tacc[k] = rows(1)
        send(tsx.at[k], trx.at[k], tx_s.at[k], tx_r.at[k], xh_peer)

    def stage_k(k):
        remote(tsx.at[k], trx.at[k], tx_s.at[k], tx_r.at[k], xh_peer).wait_recv()
        tsz[k] = (tacc[k] + trx[k].astype(F32)).astype(BF16)
        q = (pair + OFF[k]) % 4
        for v, i in enumerate(z_others(k)):
            to = at(q * 2 + i, xh, c, y, xl)
            send(tsz.at[k, i], trz.at[k, zl], tz_s.at[k, v], tz_r.at[k, zl], to)

    def stage_x():
        for a in range(3):
            for k in range(4):
                own = facz[a, k, :, :, :, cols(xh, 1024)].reshape(16, 1024)
                facd[a, 32 * k : 32 * k + 16, :] = own
                facd[a, 32 * k + 16 : 32 * k + 32, :] = fach[a, k].reshape(16, 1024)
            send(
                facd.at[a, :, cols(1 - c, 512)],
                facx.at[a],
                core_s.at[a],
                core_r.at[a],
                core_peer,
            )

    def outs(a):
        return pltpu.make_async_copy(steps.at[a], made.at[a], out_sem.at[a])

    def stage_s(part_):
        member = lax.broadcasted_iota(jnp.int32, (32, 1), 0) // 4
        if part_ == 1:
            for a in range(3):
                remote(
                    facx.at[a], facx.at[a], core_s.at[a], core_r.at[a], core_peer
                ).wait_recv()
                v = None
                for i in range(2):
                    f = facd[a, :, cols(c, 512)] if i == 0 else facx[a]
                    x = scaled[a, i]
                    w = tn(x, f) if a < 2 else tn(f, x)
                    v = w if v is None else v + w
                steps[a] = v * C_STEP
                outs(a).start()
            return
        for k in range(4):
            for i in range(2):
                core = (c + i) % 2
                q = (pair + OFF[k]) % 4
                r = jnp.zeros((32, 1), F32)
                for m in range(8):
                    who = q * 16 + (m // 2 % 2) * 8 + core * 2 + m % 2
                    who += 4 * ((xh + m // 4) % 2)
                    r = jnp.where(member == m, ranks[who].astype(F32), r)
                fit = r / (MEMBERS - 1.0) - 0.5
                for a in range(3):
                    scaled[a, i, 32 * k : 32 * k + 32, :] = (
                        in_rows(a, k, core).astype(F32) * fit
                    ).astype(BF16)

    def stage_g():
        own = pltpu.make_async_copy(tsz.at[0, zl], trz.at[0, zl], load_sem.at[13])
        own.start()
        for k in range(4):
            for i in z_others(k):
                got = trz.at[k, i]
                remote(got, got, tz_s.at[k, 0], tz_r.at[k, i], core_peer).wait_recv()
        own.wait()
        done = pltpu.make_async_copy(trz, terms, load_sem.at[14])
        done.start()
        for a in range(3):
            outs(a).wait()
        done.wait()

    stages = dict(P=stage_p, Q=stage_q, W=stage_w, T=stage_t, U=stage_u, B=stage_b)
    stages.update(C=stage_c, D=stage_d, E=stage_e, R=stage_r, F=stage_f, K=stage_k, S=stage_s)
    final = dict(X=stage_x, G=stage_g)
    for name in ORDER:
        if name[0] in stages:
            stages[name[0]](int(name[1]))
        else:
            final[name[0]]()
    for d in sent:
        d.wait_send()


def finish(terms, made, mixed, gate_step, up_step, down_step, tv, held, in_sem, sem, out_sem):
    load = pltpu.make_async_copy(terms, tv, in_sem)
    load.start()
    pieces = [(a, i, pl.ds(128 * i, 128)) for a in range(3) for i in range(4)]
    loads = [
        pltpu.make_async_copy(made.at[a, rows], held.at[a, rows], sem.at[a, i])
        for a, i, rows in pieces
    ]
    for d in loads:
        d.start()
    outs = (gate_step, up_step, down_step)
    stores = [
        pltpu.make_async_copy(held.at[a, rows], outs[a].at[rows], out_sem.at[a, i])
        for a, i, rows in pieces
    ]
    for l, d in zip(loads, stores):
        l.wait()
        d.start()
    load.wait()
    v = tv[0].astype(F32)
    for i in range(1, 8):
        v += tv[i].astype(F32)
    mixed[...] = v.astype(BF16)
    for d in stores:
        d.wait()


def local(
    tokens,
    fitness_ranks,
    gate_weight,
    up_weight,
    down_weight,
    gate_input_factor,
    up_input_factor,
    down_right,
    gate_output_factor,
    up_output_factor,
    down_left,
):
    def grouped(x):
        return x.reshape(4, 2, 2, 2, 2, RANK, 512)

    dma = pltpu.SemaphoreType.DMA
    big = jax.ShapeDtypeStruct((512, 512), F32)
    any_ = pl.BlockSpec(memory_space=pl.ANY)
    terms, made = (
        pl.pallas_call(
            kernel,
            out_shape=(
                jax.ShapeDtypeStruct((4, 2, 32, 512), BF16),
                jax.ShapeDtypeStruct((3, 512, 512), F32),
            ),
            in_specs=[pl.BlockSpec(memory_space=pltpu.SMEM)] + [any_] * 10,
            out_specs=(any_, any_),
            scratch_shapes=[
                pltpu.VMEM((512, 2048), BF16),
                pltpu.VMEM((1024, 512), BF16),
                pltpu.VMEM((4, 2, 2, 32, 512), BF16),
                pltpu.VMEM((3, 4, 2, 2, 2, 2, RANK, 512), BF16),
                pltpu.VMEM((3, 2, RANK, HIDDEN_UNITS), BF16),
                pltpu.VMEM((3, 4, 2, 2, RANK, 2048), BF16),
                pltpu.VMEM((3, 4, 2, 2, RANK, 1024), BF16),
                pltpu.VMEM((3, 128, 1024), BF16),
                pltpu.VMEM((3, 128, 512), BF16),
                pltpu.VMEM((4, 4, 2, 16, 2176), BF16),
                pltpu.VMEM((4, 3, 2, 16, 2176), BF16),
                pltpu.VMEM((4, 4, 16, 2176), BF16),
                pltpu.VMEM((4, 3, 16, 2176), BF16),
                pltpu.VMEM((4, 16, 2176), BF16),
                pltpu.VMEM((4, 16, 2176), BF16),
                pltpu.VMEM((4, 16, 2176), F32),
                pltpu.VMEM((4, 4, 2, 16, 1152), BF16),
                pltpu.VMEM((4, 2, 32, 512), BF16),
                pltpu.VMEM((4, 2, 32, 512), BF16),
                pltpu.VMEM((4, 2, 32, 512), F32),
                pltpu.VMEM((4, 2, 32, 512), BF16),
                pltpu.VMEM((4, 2, 32, 512), BF16),
                pltpu.VMEM((3, 2, 128, 512), BF16),
                pltpu.VMEM((3, 512, 512), F32),
                dma((15,)),
                dma((3,)),
                dma((3,)),
                dma((4, 2)),
                dma((4, 2)),
                dma((4,)),
                dma((4,)),
                dma((3, 4, 2)),
                dma((3, 4, 2)),
                dma((3, 4)),
                dma((3, 4)),
                dma((3,)),
                dma((3,)),
                dma((4, 3)),
                dma((4, 3)),
                dma((4,)),
                dma((4,)),
                dma((4,)),
                dma((4,)),
                dma((4, 2, 3)),
                dma((4, 2, 3)),
                dma((4,)),
                dma((4,)),
                dma((4, 2)),
                dma((4, 2)),
                dma((3,)),
            ],
            compiler_params=pltpu.CompilerParams(
                collective_id=0, has_side_effects=True, vmem_limit_bytes=56 * 2**20
            ),
        )(
            fitness_ranks,
            tokens,
            gate_weight,
            up_weight,
            down_weight,
            grouped(gate_input_factor),
            grouped(up_input_factor),
            grouped(down_right),
            gate_output_factor,
            up_output_factor,
            down_left,
        )
    )
    vmem = pl.BlockSpec(memory_space=pltpu.VMEM)
    return pl.pallas_call(
        finish,
        out_shape=(jax.ShapeDtypeStruct((32, 512), BF16), big, big, big),
        in_specs=[any_] * 2,
        out_specs=(vmem, any_, any_, any_),
        scratch_shapes=[
            pltpu.VMEM((8, 32, 512), BF16),
            pltpu.VMEM((3, 512, 512), F32),
            dma(()),
            dma((3, 4)),
            dma((3, 4)),
        ],
        compiler_params=pltpu.CompilerParams(vmem_limit_bytes=60 * 2**20),
    )(terms.reshape(8, 32, 512), made)


def solution(mesh):
    in_specs = (
        P("pop", "hid"),
        P(),
        P("hid", "pop"),
        P("hid", "pop"),
        P("pop", "hid"),
        P(None, None, "hid"),
        P(None, None, "hid"),
        P(None, None, "hid"),
        P("pop", None, None),
        P("pop", None, None),
        P("pop", None, None),
    )
    out_specs = (P("pop", "hid"), P("hid", "pop"), P("hid", "pop"), P("pop", "hid"))
    return jax.shard_map(local, mesh=mesh, in_specs=in_specs, out_specs=out_specs, check_vma=False)
```
